128 devices in a mesh: row: 8 (over x_lo, y), col: 16 (over x_hi, z, core).
Axes of the slice: x: 4 (x_hi: 2, x_lo: 2; x = x_hi * 2 + x_lo), y: 4, z: 4, core: 2. Of those that a mesh axis runs over, the one named last changes fastest.
Arguments:
- traces: bfloat16 [384, 60, 8192], P(('row', 'col')), may hold values from -80 to 80
- masks: int32 [384, 60], P(('row', 'col')), may hold values from 0 to 1, as said below
Outputs:
- correlations: float32 [384, 384, 2048], P('row', 'col')
The draws below stay inside these ranges and needn't reach their ends.
Inputs may be any that keep to these rules, and one draw needn't show every extreme that they name: `masks`: 1 marks a usable trace of a channel, 0 one left out of the stack; a channel may be flagged 0 in every trace.
All inputs are finite; a program needn't handle non-finite values.
Results may differ from the reference program's by a relative error of at most 0.0052.
Values may be sent and summed in bfloat16 or wider, within the bound.
No kernel may reach another device: no remote copies, remote signals or barrier semaphores. Data moves between devices by JAX's collectives and lax.ppermute only.
A program may use at most 320 MiB of HBM per device.

```python
import math
import jax
import jax.numpy as jnp
from jax import lax

TRACES = 60
SAMPLES = 8192
BINS = 1024
LOW_BIN = 33
LAGS = 2048
SMOOTH = 64
EDGE = 64
CHANNELS = 384


def draw_traces(key, part):
    key = jax.random.fold_in(key, 11)
    noise_key, scale_key = jax.random.split(key, 2)
    noise = jnp.clip(jax.random.normal(noise_key, (CHANNELS, TRACES, SAMPLES), jnp.float32), -5.0, 5.0)
    levels = jnp.exp(jax.random.uniform(scale_key, (CHANNELS, TRACES, 1), jnp.float32, 0.0, math.log(10.0)))
    signal = noise * levels
    return signal.astype(jnp.bfloat16)


def draw_masks(key, part):
    key = jax.random.fold_in(key, 23)
    flag_key, order_key = jax.random.split(key, 2)
    draws = jax.random.randint(flag_key, (CHANNELS, TRACES), 0, 32, jnp.int32)
    flags = jnp.minimum(draws, 1)
    dead_count = max(1, CHANNELS // 32)
    ranking = jax.random.permutation(order_key, CHANNELS).astype(jnp.int32)
    alive = (ranking >= dead_count).astype(jnp.int32)
    return flags * alive[:, None]


def setup_inputs(seed: int = 0) -> dict:
    splits = jax.random.split(jax.random.key(seed), 3)
    return {
        "traces": draw_traces(jax.random.fold_in(splits[2], 71), 0),
        "masks": draw_masks(jax.random.fold_in(splits[2], 71), 0),
    }


def dft_table():
    samples_at = jnp.arange(SAMPLES, dtype=jnp.int32)[:, None]
    passband = (LOW_BIN + jnp.arange(BINS, dtype=jnp.int32))[None, :]
    phases = samples_at * passband % SAMPLES
    angles = phases.astype(jnp.float32) * (2.0 * math.pi / SAMPLES)
    return jnp.concatenate([jnp.cos(angles), -jnp.sin(angles)], axis=1).astype(jnp.bfloat16)

def lag_table():
    passband = (LOW_BIN + jnp.arange(BINS, dtype=jnp.int32))[:, None]
    shifts = (jnp.arange(LAGS, dtype=jnp.int32) - LAGS // 2 + SAMPLES)[None, :]
    phases = passband * shifts % SAMPLES
    angles = phases.astype(jnp.float32) * (2.0 * math.pi / SAMPLES)
    factor = 2.0 / math.sqrt(BINS)
    return (factor * jnp.concatenate([jnp.cos(angles), -jnp.sin(angles)], axis=0)).astype(jnp.bfloat16)

def band_taper():
    position = jnp.arange(BINS, dtype=jnp.int32)
    distance = jnp.minimum(position, BINS - 1 - position).astype(jnp.float32)
    ramp_level = jnp.minimum((distance + 0.5) / EDGE, 1.0)
    return 0.5 - 0.5 * jnp.cos(math.pi * ramp_level)

def smoother():
    position = jnp.arange(BINS, dtype=jnp.int32)
    nearby = (jnp.abs(position[:, None] - position[None, :]) <= SMOOTH).astype(jnp.float32)
    return nearby / lax.optimization_barrier(jnp.sum(nearby, axis=0, keepdims=True))

def whiten(spectrum):
    real_part = spectrum[:, :BINS]
    imag_part = spectrum[:, BINS:]
    magnitude = jnp.sqrt(real_part * real_part + imag_part * imag_part)
    smoothed = jnp.dot(magnitude, smoother(), precision=lax.Precision.HIGHEST) + 1e-06
    weights = band_taper()[None, :] / smoothed
    return jnp.concatenate([real_part * weights, imag_part * weights], axis=1)

def reference(traces, masks):
    flat_rows = traces.reshape(CHANNELS * TRACES, SAMPLES)
    spectrum = jnp.dot(flat_rows, dft_table(), preferred_element_type=jnp.float32)
    whitened = whiten(spectrum).reshape(CHANNELS, TRACES, 2 * BINS)
    usable = masks.astype(jnp.float32)
    spectra = (whitened * usable[:, :, None]).astype(jnp.bfloat16)
    widened = spectra.astype(jnp.float32)
    all_real = widened[:, :, :BINS]
    all_imag = widened[:, :, BINS:]
    lag_matrix = lag_table()

    def one_channel(channel):
        anchor_real = lax.dynamic_index_in_dim(all_real, channel, 0, keepdims=False)
        anchor_imag = lax.dynamic_index_in_dim(all_imag, channel, 0, keepdims=False)
        anchor_mask = lax.dynamic_index_in_dim(usable, channel, 0, keepdims=False)
        cross_real = jnp.einsum('tf,btf->bf', anchor_real, all_real) + jnp.einsum('tf,btf->bf', anchor_imag, all_imag)
        cross_imag = jnp.einsum('tf,btf->bf', anchor_imag, all_real) - jnp.einsum('tf,btf->bf', anchor_real, all_imag)
        tallies = jnp.dot(usable, anchor_mask)
        stacked = (jnp.concatenate([cross_real, cross_imag], axis=1) / jnp.maximum(tallies, 1.0)[:, None]).astype(jnp.bfloat16)
        return jnp.dot(stacked, lag_matrix, preferred_element_type=jnp.float32)
    return lax.map(one_channel, jnp.arange(CHANNELS, dtype=jnp.int32))
```

```python
import math

import jax
import jax.numpy as jnp
import ml_dtypes
import numpy as np
from jax import lax
from jax.experimental import pallas as pl
from jax.experimental.pallas import tpu as pltpu
from jax.sharding import PartitionSpec as P

TRACES = 60
SAMPLES = 8192
BINS = 1024
LOW_BIN = 33
LAGS = 2048
SMOOTH = 64
EDGE = 64

F32 = jnp.float32
BF16 = jnp.bfloat16
MIB = 1 << 20

OWN = 3
SLOT = 64
QUARTER = SAMPLES // 4
CLASS = BINS // 4
PER = 8
DEVICES = BINS // PER
ROWS = 8
COLS = 16
CHANNELS = OWN * DEVICES
NT = (((1,), (1,)), ((), ()))


def bin_order():
    k = np.arange(BINS)
    return np.concatenate([k[(k + LOW_BIN) % 4 == q] for q in range(4)])


def angles_of(phases):
    return (phases % SAMPLES).astype(np.float32) * np.float32(2.0 * math.pi / SAMPLES)


def cosine(angles):
    return np.cos(angles.astype(np.float64)).astype(np.float32)


def sine(angles):
    return np.sin(angles.astype(np.float64)).astype(np.float32)


def forward_tables():
    bins = (LOW_BIN + bin_order()).reshape(4, 1, CLASS)
    angles = angles_of(np.arange(QUARTER).reshape(1, QUARTER, 1) * bins)
    return np.concatenate([cosine(angles), -sine(angles)], axis=2).astype(ml_dtypes.bfloat16)


def lag_table():
    bins = (LOW_BIN + bin_order()).reshape(DEVICES, PER, 1)
    angles = angles_of(bins * (np.arange(LAGS) - LAGS // 2 + SAMPLES).reshape(1, 1, LAGS))
    both = np.stack([cosine(angles), -sine(angles)], axis=1) * np.float32(2.0 / math.sqrt(BINS))
    return both.reshape(2 * BINS, LAGS).astype(ml_dtypes.bfloat16)


def window_tables():
    order = bin_order()
    nearby = np.abs(order[:, None] - order[None, :]) <= SMOOTH
    distance = np.minimum(order, BINS - 1 - order).astype(np.float32)
    ramp = np.minimum((distance + np.float32(0.5)) / np.float32(EDGE), np.float32(1.0))
    taper = np.float32(0.5) - np.float32(0.5) * cosine(np.float32(math.pi) * ramp)
    rows = np.zeros((8, BINS), np.float32)
    rows[0] = taper
    rows[1] = np.float32(1.0) / nearby.sum(axis=0).astype(np.float32)
    return nearby.astype(ml_dtypes.bfloat16), rows


def iota(shape, axis):
    return lax.broadcasted_iota(jnp.int32, shape, axis)


def halves(value):
    high = value.astype(BF16)
    return high, (value - high.astype(F32)).astype(BF16)


def whiten_kernel(x_ref, m_ref, table_ref, near_ref, rows_ref, out_ref, u_ref, re_ref, im_ref):
    q = pl.program_id(0)
    span = OWN * SLOT

    @pl.when(q == 0)
    def fold():
        for i in range(OWN):
            part = [
                x_ref[i, :, QUARTER * j : QUARTER * (j + 1)].astype(F32) for j in range(4)
            ]
            even, odd = part[0] + part[2], part[1] + part[3]
            kinds = (even + odd, even - odd, part[0] - part[2], part[1] - part[3])
            for kind, value in enumerate(kinds):
                high, low = halves(value)
                u_ref[kind, SLOT * i : SLOT * i + TRACES, :] = high
                u_ref[kind, span + SLOT * i : span + SLOT * i + TRACES, :] = low

    def times_table(kind):
        both = jnp.dot(u_ref[kind], table_ref[0], preferred_element_type=F32)
        return both[:span] + both[span:]

    @pl.when(q % 2 == 0)
    def real_class():
        both = times_table(q // 2)
        re_ref[q] = both[:, :CLASS]
        im_ref[q] = both[:, CLASS:]

    @pl.when(q % 2 == 1)
    def complex_class():
        sign = (2 - q).astype(F32)
        first, second = times_table(2), times_table(3)
        re_ref[q] = first[:, :CLASS] + sign * second[:, CLASS:]
        im_ref[q] = first[:, CLASS:] - sign * second[:, :CLASS]

    @pl.when(q == 3)
    def whiten():
        real = jnp.concatenate([re_ref[c] for c in range(4)], axis=1)
        imag = jnp.concatenate([im_ref[c] for c in range(4)], axis=1)
        magnitude = jnp.sqrt(real * real + imag * imag)
        high, low = halves(magnitude)
        near = near_ref[...]
        total = jnp.dot(high, near, preferred_element_type=F32) + jnp.dot(
            low, near, preferred_element_type=F32
        )
        level = total * rows_ref[1:2, :] + 1e-06
        weights = rows_ref[0:1, :] / level
        real = real * weights
        imag = imag * weights
        pieces = []
        for i in range(OWN):
            flags = m_ref[i : i + 1, :].astype(F32)
            square = (SLOT, TRACES)
            diagonal = iota(square, 0) == iota(square, 1)
            usable = jnp.sum(jnp.where(diagonal, flags, 0.0), axis=1, keepdims=True) > 0.5
            own_real = jnp.where(usable, real[SLOT * i : SLOT * (i + 1)], 0.0)
            own_imag = jnp.where(usable, imag[SLOT * i : SLOT * (i + 1)], 0.0)
            trace = iota((8, TRACES), 1)
            row = iota((8, TRACES), 0)
            spread = (
                (iota((TRACES, 128), 0) >> 3) == (iota((TRACES, 128), 1) & 7)
            ).astype(BF16)
            spare = []
            for shift in (4, 0):
                chosen = jnp.where((trace & 7) == ((row + shift) & 7), flags, 0.0)
                placed = jnp.dot(chosen.astype(BF16), spread, preferred_element_type=F32)
                spare.append(jnp.concatenate([placed] * (BINS // 128), axis=1))
            last = iota((8, BINS), 0) >= 4
            stack = jnp.concatenate(
                [
                    own_real[: SLOT - 8],
                    jnp.where(last, spare[0], own_real[SLOT - 8 :]),
                    own_imag[: SLOT - 8],
                    jnp.where(last, spare[1], own_imag[SLOT - 8 :]),
                ],
                axis=0,
            )
            pieces.append(jnp.transpose(stack).reshape(DEVICES, PER, 2 * SLOT))
        out_ref[...] = jnp.concatenate(pieces, axis=1).astype(BF16)


def whitened_spectra(traces, masks):
    near, rows = window_tables()
    return pl.pallas_call(
        whiten_kernel,
        grid=(4,),
        in_specs=[
            pl.BlockSpec((OWN, TRACES, SAMPLES), lambda q: (0, 0, 0)),
            pl.BlockSpec((OWN, TRACES), lambda q: (0, 0)),
            pl.BlockSpec((1, QUARTER, 2 * CLASS), lambda q: (q, 0, 0)),
            pl.BlockSpec((BINS, BINS), lambda q: (0, 0)),
            pl.BlockSpec((8, BINS), lambda q: (0, 0)),
        ],
        out_specs=pl.BlockSpec((DEVICES, OWN * PER, 2 * SLOT), lambda q: (0, 0, 0)),
        out_shape=jax.ShapeDtypeStruct((DEVICES, OWN * PER, 2 * SLOT), BF16),
        scratch_shapes=[
            pltpu.VMEM((4, 2 * OWN * SLOT, QUARTER), BF16),
            pltpu.VMEM((4, OWN * SLOT, CLASS), F32),
            pltpu.VMEM((4, OWN * SLOT, CLASS), F32),
        ],
        compiler_params=pltpu.CompilerParams(vmem_limit_bytes=48 * MIB),
        name="whiten",
    )(traces, masks, jnp.asarray(forward_tables()), jnp.asarray(near), jnp.asarray(rows))


def cross_kernel(got_ref, out_ref, own_ref, right_ref, flag_ref, part_ref):
    lanes = 2 * SLOT
    block = CHANNELS // COLS
    own_ref[...] = got_ref[...].reshape(DEVICES * OWN * PER, lanes).astype(F32)
    for i in range(OWN):
        for j in range(PER):
            value = own_ref[pl.ds(i * PER + j, DEVICES, stride=OWN * PER), :]
            for half in range(2):
                right_ref[j, pl.ds(half * CHANNELS + i, DEVICES, stride=OWN), :] = value
    lane = iota((CHANNELS, lanes), 1)
    spare = (lane & (SLOT - 1)) >= TRACES
    flags = jnp.zeros((CHANNELS, lanes), F32)
    for j in range(PER):
        value = jnp.where(spare, right_ref[j, :CHANNELS, :], 0.0)
        flags += pltpu.roll(value, 4 * j, 1) if j else value
    flag_ref[:CHANNELS] = flags
    flag_ref[CHANNELS:] = flags

    tile = (PER, lanes)
    row = iota(tile, 0)
    kept = (iota(tile, 1) & (SLOT - 1)) < TRACES
    sign = jnp.where(iota(tile, 1) < SLOT, 1.0, -1.0)

    def one_source(s, carry):
        start = pl.multiple_of((COLS - s) * block, 8)
        right = jnp.concatenate(
            [right_ref[j, pl.ds(start, CHANNELS), :] for j in range(PER)], axis=1
        ).astype(BF16)
        right_flags = flag_ref[pl.ds(start, CHANNELS), :].astype(BF16)
        left, left_flags = [], []
        for i in range(OWN):
            for r in range(ROWS):
                first = pl.multiple_of((r * COLS + s) * OWN * PER + i * PER, 8)
                value = jnp.where(kept, own_ref[pl.ds(first, PER), :], 0.0)
                turned = pltpu.roll(value, SLOT, 1) * sign
                both = []
                for j in range(PER):
                    keep = row == j
                    both.append(
                        jnp.concatenate(
                            [jnp.where(keep, value, 0.0), jnp.where(keep, turned, 0.0)], axis=0
                        )
                    )
                left.append(jnp.concatenate(both, axis=1).astype(BF16))
            left_flags.append(flag_ref[pl.ds(OWN * s + i, ROWS, stride=OWN * COLS), :])
        cross = lax.dot_general(
            jnp.concatenate(left, axis=0), right, NT, preferred_element_type=F32
        )
        tallies = lax.dot_general(
            jnp.concatenate(left_flags, axis=0).astype(BF16),
            right_flags,
            NT,
            preferred_element_type=F32,
        )
        scale = 1.0 / jnp.maximum(tallies, 1.0)
        stacked = cross.reshape(OWN * ROWS, 2 * PER, CHANNELS) * scale[:, None, :]
        part_ref[s] = stacked.astype(BF16)
        return carry

    lax.fori_loop(0, COLS, one_source, 0)

    where = iota((2 * PER, CHANNELS), 1) // block

    def one_row(g, carry):
        i = g // ROWS
        r = g % ROWS
        parts = [part_ref[s, g] for s in range(COLS)]
        for c in range(COLS):
            tiles = []
            for t in range(CHANNELS // 128):
                cut = slice(128 * t, 128 * (t + 1))
                places = range(128 * t // block, (128 * (t + 1) - 1) // block + 1)
                value = parts[(places[0] - c) % COLS][:, cut]
                for place in places[1:]:
                    value = jnp.where(
                        where[:, cut] == place, parts[(place - c) % COLS][:, cut], value
                    )
                tiles.append(value)
            lanes_of = pl.ds(pl.multiple_of(i * CHANNELS, 128), CHANNELS)
            out_ref[r * COLS + c, :, lanes_of] = jnp.concatenate(tiles, axis=1)
        return carry

    lax.fori_loop(0, OWN * ROWS, one_row, 0)


def cross_spectra(got):
    return pl.pallas_call(
        cross_kernel,
        out_shape=jax.ShapeDtypeStruct((DEVICES, 2 * PER, OWN * CHANNELS), BF16),
        scratch_shapes=[
            pltpu.VMEM((DEVICES * OWN * PER, 2 * SLOT), F32),
            pltpu.VMEM((PER, 2 * CHANNELS, 2 * SLOT), F32),
            pltpu.VMEM((2 * CHANNELS, 2 * SLOT), F32),
            pltpu.VMEM((COLS, OWN * ROWS, 2 * PER, CHANNELS), BF16),
        ],
        compiler_params=pltpu.CompilerParams(vmem_limit_bytes=48 * MIB),
        name="cross",
    )(got)


LAG_STEP = 512


def lag_kernel(col_ref, x_ref, table_ref, out_ref):
    block = CHANNELS // COLS
    turned = jnp.transpose(x_ref[...])

    def one_step(n, carry):
        lags = pl.ds(pl.multiple_of(n * LAG_STEP, LAG_STEP), LAG_STEP)
        value = jnp.dot(turned, table_ref[:, lags], preferred_element_type=F32)
        for place in range(COLS):
            source = (place + COLS - col_ref[0]) % COLS
            out_ref[source, 0, :, lags] = value[block * place : block * (place + 1)]
        return carry

    lax.fori_loop(0, LAGS // LAG_STEP, one_step, 0)


def correlations_of(stacked, col):
    block = CHANNELS // COLS
    return pl.pallas_call(
        lag_kernel,
        grid_spec=pltpu.PrefetchScalarGridSpec(
            num_scalar_prefetch=1,
            grid=(OWN,),
            in_specs=[
                pl.BlockSpec((2 * BINS, CHANNELS), lambda i, col: (0, i)),
                pl.BlockSpec((2 * BINS, LAGS), lambda i, col: (0, 0)),
            ],
            out_specs=pl.BlockSpec((COLS, 1, block, LAGS), lambda i, col: (0, i, 0, 0)),
        ),
        out_shape=jax.ShapeDtypeStruct((COLS, OWN, block, LAGS), F32),
        compiler_params=pltpu.CompilerParams(vmem_limit_bytes=48 * MIB),
        name="lags",
    )(col, stacked, jnp.asarray(lag_table()))


def local(traces, masks):
    axes = ("row", "col")
    spectra = whitened_spectra(traces, masks)
    by_bin = lax.all_to_all(spectra, axes, 0, 0, tiled=True)
    stacked = cross_spectra(by_bin)
    by_pair = lax.all_to_all(stacked, axes, 0, 0, tiled=True)
    col = lax.axis_index("col").astype(jnp.int32).reshape(1)
    result = correlations_of(by_pair.reshape(2 * BINS, OWN * CHANNELS), col)
    return result.reshape(OWN * COLS, CHANNELS // COLS, LAGS)


def solution(mesh):
    in_specs = (P(("row", "col"), None, None), P(("row", "col"), None))
    out_specs = P("row", "col", None)
    return jax.shard_map(local, mesh=mesh, in_specs=in_specs, out_specs=out_specs, check_vma=False)
```

```python
import math

import jax
import jax.numpy as jnp
import ml_dtypes
import numpy as np
from jax import lax
from jax.experimental import pallas as pl
from jax.experimental.pallas import tpu as pltpu
from jax.sharding import PartitionSpec as P

TRACES = 60
SAMPLES = 8192
BINS = 1024
LOW_BIN = 33
LAGS = 2048
SMOOTH = 64
EDGE = 64

F32 = jnp.float32
BF16 = jnp.bfloat16
MIB = 1 << 20

OWN = 3
SLOT = 64
QUARTER = SAMPLES // 4
CLASS = BINS // 4
PER = 8
DEVICES = BINS // PER
ROWS = 8
COLS = 16
CHANNELS = OWN * DEVICES
NT = (((1,), (1,)), ((), ()))


def bin_order():
    k = np.arange(BINS)
    return np.concatenate([k[(k + LOW_BIN) % 4 == q] for q in range(4)])


def angles_of(phases):
    return (phases % SAMPLES).astype(np.float32) * np.float32(2.0 * math.pi / SAMPLES)


def cosine(angles):
    return np.cos(angles.astype(np.float64)).astype(np.float32)


def sine(angles):
    return np.sin(angles.astype(np.float64)).astype(np.float32)


def forward_tables():
    bins = (LOW_BIN + bin_order()).reshape(4, 1, CLASS)
    angles = angles_of(np.arange(QUARTER).reshape(1, QUARTER, 1) * bins)
    return np.concatenate([cosine(angles), -sine(angles)], axis=2).astype(ml_dtypes.bfloat16)


def lag_tables():
    bins = LOW_BIN + bin_order()
    factor = np.float32(2.0 / math.sqrt(BINS))

    def at(lags):
        angles = angles_of(bins[:, None] * (lags[None, :] + SAMPLES))
        both = factor * np.stack([cosine(angles), -sine(angles)])
        return both.astype(ml_dtypes.bfloat16)

    edge = np.zeros((8, BINS), np.float32)
    edge[:2] = at(np.array([-LAGS // 2]))[:, :, 0].astype(np.float32)
    return at(np.arange(LAGS // 2)), edge


def window_tables():
    order = bin_order()
    nearby = np.abs(order[:, None] - order[None, :]) <= SMOOTH
    distance = np.minimum(order, BINS - 1 - order).astype(np.float32)
    ramp = np.minimum((distance + np.float32(0.5)) / np.float32(EDGE), np.float32(1.0))
    taper = np.float32(0.5) - np.float32(0.5) * cosine(np.float32(math.pi) * ramp)
    rows = np.zeros((8, BINS), np.float32)
    rows[0] = taper
    rows[1] = np.float32(1.0) / nearby.sum(axis=0).astype(np.float32)
    return nearby.astype(ml_dtypes.bfloat16), rows


def iota(shape, axis):
    return lax.broadcasted_iota(jnp.int32, shape, axis)


def halves(value):
    high = value.astype(BF16)
    return high, (value - high.astype(F32)).astype(BF16)


def whiten_kernel(
    x_hbm, m_hbm, table_hbm, near_hbm, rows_hbm, out_ref, x_ref, m_ref, table_ref, near_ref, rows_ref, u_ref, sems
):
    span = OWN * SLOT
    order = (0, 2, 1, 3)
    x_copies = [
        pltpu.make_async_copy(x_hbm.at[i], x_ref.at[i], sems.at[i]) for i in range(OWN)
    ]
    table_copies = {
        q: pltpu.make_async_copy(table_hbm.at[q], table_ref.at[q], sems.at[OWN + q]) for q in order
    }
    last_copies = [
        pltpu.make_async_copy(m_hbm, m_ref, sems.at[7]),
        pltpu.make_async_copy(rows_hbm, rows_ref, sems.at[8]),
        pltpu.make_async_copy(near_hbm, near_ref, sems.at[9]),
    ]
    for copy in (*x_copies, *table_copies.values(), *last_copies):
        copy.start()

    for i in range(OWN):
        x_copies[i].wait()
        part = [x_ref[i, :, QUARTER * j : QUARTER * (j + 1)].astype(F32) for j in range(4)]
        even, odd = part[0] + part[2], part[1] + part[3]
        kinds = (even + odd, even - odd, part[0] - part[2], part[1] - part[3])
        for kind, value in enumerate(kinds):
            high, low = halves(value)
            u_ref[kind, SLOT * i : SLOT * i + TRACES, :] = high
            u_ref[kind, span + SLOT * i : span + SLOT * i + TRACES, :] = low

    def times_table(kind, q):
        both = jnp.dot(u_ref[kind], table_ref[q], preferred_element_type=F32)
        both = both[:span] + both[span:]
        return both[:, :CLASS], both[:, CLASS:]

    reals, imags = {}, {}
    for q in order:
        table_copies[q].wait()
        if q % 2 == 0:
            reals[q], imags[q] = times_table(q // 2, q)
        else:
            first, second = times_table(2, q), times_table(3, q)
            if q == 1:
                reals[q], imags[q] = first[0] + second[1], first[1] - second[0]
            else:
                reals[q], imags[q] = first[0] - second[1], first[1] + second[0]
    for copy in last_copies:
        copy.wait()

    real = jnp.concatenate([reals[q] for q in range(4)], axis=1)
    imag = jnp.concatenate([imags[q] for q in range(4)], axis=1)
    magnitude = jnp.sqrt(real * real + imag * imag)
    near = near_ref[...]
    both = jnp.dot(
        jnp.concatenate(halves(magnitude), axis=0), near, preferred_element_type=F32
    )
    level = (both[:span] + both[span:]) * rows_ref[1:2, :] + 1e-06
    weights = rows_ref[0:1, :] / level
    real = real * weights
    imag = imag * weights
    pieces = []
    for i in range(OWN):
        flags = m_ref[i : i + 1, :].astype(F32)
        square = (SLOT, TRACES)
        diagonal = iota(square, 0) == iota(square, 1)
        usable = jnp.sum(jnp.where(diagonal, flags, 0.0), axis=1, keepdims=True) > 0.5
        own_real = jnp.where(usable, real[SLOT * i : SLOT * (i + 1)], 0.0)
        own_imag = jnp.where(usable, imag[SLOT * i : SLOT * (i + 1)], 0.0)
        trace = iota((8, TRACES), 1)
        row = iota((8, TRACES), 0)
        spread = ((iota((TRACES, 128), 0) >> 3) == (iota((TRACES, 128), 1) & 7)).astype(BF16)
        spare = []
        for shift in (4, 0):
            chosen = jnp.where((trace & 7) == ((row + shift) & 7), flags, 0.0)
            placed = jnp.dot(chosen.astype(BF16), spread, preferred_element_type=F32)
            spare.append(jnp.concatenate([placed] * (BINS // 128), axis=1))
        last = iota((8, BINS), 0) >= 4
        stack = jnp.concatenate(
            [
                own_real[: SLOT - 8],
                jnp.where(last, spare[0], own_real[SLOT - 8 :]),
                own_imag[: SLOT - 8],
                jnp.where(last, spare[1], own_imag[SLOT - 8 :]),
            ],
            axis=0,
        )
        pieces.append(jnp.transpose(stack).reshape(DEVICES, PER, 2 * SLOT))
    out_ref[...] = jnp.concatenate(pieces, axis=1).astype(BF16)


def anywhere(count):
    return [pl.BlockSpec(memory_space=pl.ANY)] * count


def whitened_spectra(traces, masks):
    near, rows = window_tables()
    return pl.pallas_call(
        whiten_kernel,
        in_specs=anywhere(5),
        out_shape=jax.ShapeDtypeStruct((DEVICES, OWN * PER, 2 * SLOT), BF16),
        scratch_shapes=[
            pltpu.VMEM((OWN, TRACES, SAMPLES), BF16),
            pltpu.VMEM((OWN, TRACES), jnp.int32),
            pltpu.VMEM((4, QUARTER, 2 * CLASS), BF16),
            pltpu.VMEM((BINS, BINS), BF16),
            pltpu.VMEM((8, BINS), F32),
            pltpu.VMEM((4, 2 * OWN * SLOT, QUARTER), BF16),
            pltpu.SemaphoreType.DMA((10,)),
        ],
        compiler_params=pltpu.CompilerParams(vmem_limit_bytes=60 * MIB),
        name="whiten",
    )(traces, masks, jnp.asarray(forward_tables()), jnp.asarray(near), jnp.asarray(rows))


def cross_kernel(got_ref, out_hbm, own_ref, sorted_ref, scale_ref, part_ref, merged_ref, sems):
    lanes = 2 * SLOT
    block = CHANNELS // COLS
    own_ref[...] = got_ref[...].reshape(DEVICES * OWN * PER, lanes).astype(F32)
    lane = iota((CHANNELS, lanes), 1)
    spare = (lane & (SLOT - 1)) >= TRACES
    sign = jnp.where(lane < SLOT, 1.0, -1.0)
    flags = jnp.zeros((CHANNELS, lanes), F32)
    for j in range(PER):
        for i in range(OWN):
            value = own_ref[pl.ds(i * PER + j, DEVICES, stride=OWN * PER), :]
            sorted_ref[j, pl.ds(i, DEVICES, stride=OWN), :] = value
        extra = jnp.where(spare, sorted_ref[j], 0.0)
        flags += pltpu.roll(extra, 4 * j, 1) if j else extra
    flags = flags.astype(BF16)
    tallies = lax.dot_general(flags, flags, NT, preferred_element_type=F32)
    scale_ref[...] = 1.0 / jnp.maximum(tallies, 1.0)
    for j in range(PER):
        right = sorted_ref[j]
        left = jnp.where(spare, 0.0, right)
        left = jnp.concatenate([left, pltpu.roll(left, SLOT, 1) * sign], axis=0)
        cross = lax.dot_general(
            left.astype(BF16), right.astype(BF16), NT, preferred_element_type=F32
        )
        for t in range(CHANNELS // 128):
            for p in range(2):
                part_ref[t, pl.ds(PER * p + j, CHANNELS, stride=2 * PER), :] = (
                    cross[CHANNELS * p : CHANNELS * (p + 1), 128 * t : 128 * (t + 1)]
                    * scale_ref[:, 128 * t : 128 * (t + 1)]
                )

    def copy_out(g):
        return pltpu.make_async_copy(
            merged_ref.at[g],
            out_hbm.at[
                pl.ds((g % ROWS) * COLS, COLS),
                :,
                pl.ds(pl.multiple_of(g // ROWS * CHANNELS, 128), CHANNELS),
            ],
            sems.at[g],
        )

    where = iota((2 * PER, CHANNELS), 1) // block
    bits = [(where >> k) & 1 == 1 for k in range(4)]

    def one_row(g, carry):
        parts = []
        for s in range(COLS):
            channel = (g % ROWS) * OWN * COLS + OWN * s + g // ROWS
            rows = pl.ds(pl.multiple_of(channel * 2 * PER, 2 * PER), 2 * PER)
            value = jnp.concatenate(
                [part_ref[t, rows, :] for t in range(CHANNELS // 128)], axis=1
            )
            value = value.astype(BF16)
            parts.append(pltpu.roll(value, block * s, 1) if s else value)
        for t in range(CHANNELS // 128):
            cut = slice(128 * t, 128 * (t + 1))
            tiles = [part[:, cut] for part in parts]
            for k in range(4):
                tiles = [
                    jnp.where(bits[k][:, cut], tiles[(s + (1 << k)) % COLS], tiles[s])
                    for s in range(COLS)
                ]
            for c in range(COLS):
                merged_ref[g, c, :, cut] = tiles[-c % COLS]
        copy_out(g).start()
        return carry

    lax.fori_loop(0, OWN * ROWS, one_row, 0, unroll=3)

    def one_wait(g, carry):
        copy_out(g).wait()
        return carry

    lax.fori_loop(0, OWN * ROWS, one_wait, 0)


def cross_spectra(got):
    return pl.pallas_call(
        cross_kernel,
        out_specs=pl.BlockSpec(memory_space=pl.ANY),
        out_shape=jax.ShapeDtypeStruct((DEVICES, 2 * PER, OWN * CHANNELS), BF16),
        scratch_shapes=[
            pltpu.VMEM((DEVICES * OWN * PER, 2 * SLOT), F32),
            pltpu.VMEM((PER, CHANNELS, 2 * SLOT), F32),
            pltpu.VMEM((CHANNELS, CHANNELS), F32),
            pltpu.VMEM((CHANNELS // 128, CHANNELS * 2 * PER, 128), F32),
            pltpu.VMEM((OWN * ROWS, COLS, 2 * PER, CHANNELS), BF16),
            pltpu.SemaphoreType.DMA((OWN * ROWS,)),
        ],
        compiler_params=pltpu.CompilerParams(vmem_limit_bytes=60 * MIB),
        name="cross",
    )(got)


LAG_STEP = 256
HALF = LAGS // 2


def lag_kernel(col_ref, x_hbm, table_hbm, edge_ref, out_hbm, x_ref, table_ref, out_ref, sems):
    block = CHANNELS // COLS
    steps = HALF // LAG_STEP
    x_copies = [
        pltpu.make_async_copy(
            x_hbm.at[:, :, pl.ds(CHANNELS * i, CHANNELS)], x_ref.at[i], sems.at[i]
        )
        for i in range(OWN)
    ]
    table_copies = [
        pltpu.make_async_copy(table_hbm.at[n], table_ref.at[n], sems.at[OWN + n])
        for n in range(steps)
    ]
    x_copies[0].start()
    for n in reversed(range(steps)):
        table_copies[n].start()
    for i in range(1, OWN):
        x_copies[i].start()

    def store(i, first, value):
        width = value.shape[1]
        for place in range(COLS):
            source = (place + COLS - col_ref[0]) % COLS
            out_ref[i, source, :, first : first + width] = value[block * place : block * (place + 1)]

    copies = []

    def send(i, first):
        copy = pltpu.make_async_copy(
            out_ref.at[i, :, :, pl.ds(first, LAG_STEP)],
            out_hbm.at[:, i, :, pl.ds(first, LAG_STEP)],
            sems.at[OWN + steps + len(copies)],
        )
        copy.start()
        copies.append(copy)

    lane = iota((CHANNELS, 128), 1)
    mirror = (128 - lane) & 127
    for i in range(OWN):
        x_copies[i].wait()
        parts = []
        for p in range(2):
            rows = x_ref[i, :, PER * p : PER * (p + 1), :].astype(F32).reshape(BINS, CHANNELS)
            parts.append(jnp.transpose(rows))
        edge = jnp.sum(
            parts[0] * edge_ref[0:1, :] + parts[1] * edge_ref[1:2, :], axis=1, keepdims=True
        )
        real, imag = parts[0].astype(BF16), parts[1].astype(BF16)
        before = jnp.broadcast_to(edge, (CHANNELS, 128))
        for n in reversed(range(steps)):
            if i == 0:
                table_copies[n].wait()
            even = jnp.dot(real, table_ref[n, 0], preferred_element_type=F32)
            odd = jnp.dot(imag, table_ref[n, 1], preferred_element_type=F32)
            store(i, HALF + LAG_STEP * n, even + odd)
            send(i, HALF + LAG_STEP * n)
            back = even - odd
            for t in reversed(range(LAG_STEP // 128)):
                turned = jnp.take_along_axis(back[:, 128 * t : 128 * (t + 1)], mirror, axis=1)
                first = HALF - LAG_STEP * n - 128 * (t + 1)
                store(i, first, jnp.where(lane == 0, before, turned))
                before = turned
            send(i, HALF - LAG_STEP * (n + 1))
    for copy in copies:
        copy.wait()


def correlations_of(stacked, col):
    block = CHANNELS // COLS
    steps = HALF // LAG_STEP
    table, edge = lag_tables()
    table = table.reshape(2, BINS, steps, LAG_STEP).transpose(2, 0, 1, 3)
    return pl.pallas_call(
        lag_kernel,
        in_specs=[
            pl.BlockSpec(memory_space=pltpu.SMEM),
            *anywhere(2),
            pl.BlockSpec(memory_space=pltpu.VMEM),
        ],
        out_specs=pl.BlockSpec(memory_space=pl.ANY),
        out_shape=jax.ShapeDtypeStruct((COLS, OWN, block, LAGS), F32),
        scratch_shapes=[
            pltpu.VMEM((OWN, DEVICES, 2 * PER, CHANNELS), BF16),
            pltpu.VMEM((steps, 2, BINS, LAG_STEP), BF16),
            pltpu.VMEM((OWN, COLS, block, LAGS), F32),
            pltpu.SemaphoreType.DMA((OWN + steps + 2 * OWN * steps,)),
        ],
        compiler_params=pltpu.CompilerParams(vmem_limit_bytes=60 * MIB),
        name="lags",
    )(col, stacked, jnp.asarray(table), jnp.asarray(edge))


def local(traces, masks):
    axes = ("row", "col")
    spectra = whitened_spectra(traces, masks)
    by_bin = lax.all_to_all(spectra, axes, 0, 0, tiled=True)
    stacked = cross_spectra(by_bin)
    by_pair = lax.all_to_all(stacked, axes, 0, 0, tiled=True)
    col = lax.axis_index("col").astype(jnp.int32).reshape(1)
    result = correlations_of(by_pair, col)
    return result.reshape(OWN * COLS, CHANNELS // COLS, LAGS)


def solution(mesh):
    in_specs = (P(("row", "col"), None, None), P(("row", "col"), None))
    out_specs = P("row", "col", None)
    return jax.shard_map(local, mesh=mesh, in_specs=in_specs, out_specs=out_specs, check_vma=False)
```

```python
import math

import jax
import jax.numpy as jnp
import ml_dtypes
import numpy as np
from jax import lax
from jax.experimental import pallas as pl
from jax.experimental.pallas import tpu as pltpu
from jax.sharding import PartitionSpec as P

TRACES = 60
SAMPLES = 8192
BINS = 1024
LOW_BIN = 33
LAGS = 2048
SMOOTH = 64
EDGE = 64

F32 = jnp.float32
BF16 = jnp.bfloat16
MIB = 1 << 20

OWN = 3
SLOT = 64
QUARTER = SAMPLES // 4
CLASS = BINS // 4
PER = 8
DEVICES = BINS // PER
ROWS = 8
COLS = 16
CHANNELS = OWN * DEVICES
NT = (((1,), (1,)), ((), ()))


def bin_order():
    k = np.arange(BINS)
    return np.concatenate([k[(k + LOW_BIN) % 4 == q] for q in range(4)])


def angles_of(phases):
    return (phases % SAMPLES).astype(np.float32) * np.float32(2.0 * math.pi / SAMPLES)


def cosine(angles):
    return np.cos(angles.astype(np.float64)).astype(np.float32)


def sine(angles):
    return np.sin(angles.astype(np.float64)).astype(np.float32)


def forward_tables():
    bins = (LOW_BIN + bin_order()).reshape(4, 1, CLASS)
    angles = angles_of(np.arange(QUARTER).reshape(1, QUARTER, 1) * bins)
    return np.concatenate([cosine(angles), -sine(angles)], axis=2).astype(ml_dtypes.bfloat16)


def lag_tables():
    bins = LOW_BIN + bin_order()
    factor = np.float32(2.0 / math.sqrt(BINS))

    def at(lags):
        angles = angles_of(bins[:, None] * (lags[None, :] + SAMPLES))
        both = factor * np.stack([cosine(angles), -sine(angles)])
        return both.astype(ml_dtypes.bfloat16)

    edge = np.zeros((8, BINS), np.float32)
    edge[:2] = at(np.array([-LAGS // 2]))[:, :, 0].astype(np.float32)
    return at(np.arange(LAGS // 2)), edge


def window_rows():
    order = bin_order()
    nearby = np.abs(order[:, None] - order[None, :]) <= SMOOTH
    distance = np.minimum(order, BINS - 1 - order).astype(np.float32)
    ramp = np.minimum((distance + np.float32(0.5)) / np.float32(EDGE), np.float32(1.0))
    taper = np.float32(0.5) - np.float32(0.5) * cosine(np.float32(math.pi) * ramp)
    rows = np.zeros((8, BINS), np.float32)
    rows[0] = taper
    rows[1] = np.float32(1.0) / nearby.sum(axis=0).astype(np.float32)
    return rows


def iota(shape, axis):
    return lax.broadcasted_iota(jnp.int32, shape, axis)


def halves(value):
    high = value.astype(BF16)
    return high, (value - high.astype(F32)).astype(BF16)


def whiten_kernel(
    x_hbm, m_hbm, table_hbm, rows_hbm, out_ref, x_ref, m_ref, table_ref, rows_ref, u_ref, sems
):
    span = OWN * SLOT
    order = (0, 2, 1, 3)
    x_copies = [
        pltpu.make_async_copy(x_hbm.at[i], x_ref.at[i], sems.at[i]) for i in range(OWN)
    ]
    table_copies = {
        q: pltpu.make_async_copy(table_hbm.at[q], table_ref.at[q], sems.at[OWN + q]) for q in order
    }
    last_copies = [
        pltpu.make_async_copy(m_hbm, m_ref, sems.at[7]),
        pltpu.make_async_copy(rows_hbm, rows_ref, sems.at[8]),
    ]
    for copy in (*x_copies, *table_copies.values(), *last_copies):
        copy.start()
    for copy in x_copies:
        copy.wait()

    for i in range(OWN):
        part = [x_ref[i, :, QUARTER * j : QUARTER * (j + 1)].astype(F32) for j in range(4)]
        even, odd = part[0] + part[2], part[1] + part[3]
        kinds = (even + odd, even - odd, part[0] - part[2], part[1] - part[3])
        for kind, value in enumerate(kinds):
            high, low = halves(value)
            u_ref[kind, SLOT * i : SLOT * i + TRACES, :] = high
            u_ref[kind, span + SLOT * i : span + SLOT * i + TRACES, :] = low

    def times_table(kind, q):
        both = jnp.dot(u_ref[kind], table_ref[q], preferred_element_type=F32)
        both = both[:span] + both[span:]
        return both[:, :CLASS], both[:, CLASS:]

    reals, imags = {}, {}
    for q in order:
        if q == 0:
            table_copies[0].wait()
            table_copies[2].wait()
        if q == 1:
            for copy in (table_copies[1], table_copies[3], *last_copies):
                copy.wait()
        if q % 2 == 0:
            reals[q], imags[q] = times_table(q // 2, q)
        else:
            first, second = times_table(2, q), times_table(3, q)
            if q == 1:
                reals[q], imags[q] = first[0] + second[1], first[1] - second[0]
            else:
                reals[q], imags[q] = first[0] - second[1], first[1] + second[0]

    place = {c: (c - LOW_BIN) % 4 for c in range(4)}
    by_place = sorted(range(4), key=place.get)
    sizes = {c: jnp.sqrt(reals[c] * reals[c] + imags[c] * imags[c]) for c in range(4)}
    every = sizes[0] + sizes[1] + sizes[2] + sizes[3]
    reach = SMOOTH // 4
    band = jnp.abs(iota((CLASS, CLASS), 0) - iota((CLASS, CLASS), 1)) < reach
    middle = jnp.dot(
        jnp.concatenate(halves(every), axis=0), band.astype(BF16), preferred_element_type=F32
    )
    middle = middle[:span] + middle[span:]
    lane = iota((span, CLASS), 1)
    totals = {}
    upto = jnp.zeros((span, CLASS), F32)
    for c in by_place:
        onward = every - upto
        upto = upto + sizes[c]
        ahead = jnp.where(lane < CLASS - reach, pltpu.roll(upto, CLASS - reach, 1), 0.0)
        behind = jnp.where(lane >= reach, pltpu.roll(onward, reach, 1), 0.0)
        totals[c] = middle + ahead + behind
    total = jnp.concatenate([totals[c] for c in range(4)], axis=1)
    real = jnp.concatenate([reals[q] for q in range(4)], axis=1)
    imag = jnp.concatenate([imags[q] for q in range(4)], axis=1)
    level = total * rows_ref[1:2, :] + 1e-06
    weights = rows_ref[0:1, :] / level
    real = real * weights
    imag = imag * weights
    pieces = []
    for i in range(OWN):
        flags = m_ref[i : i + 1, :].astype(F32)
        square = (SLOT, TRACES)
        diagonal = iota(square, 0) == iota(square, 1)
        usable = jnp.sum(jnp.where(diagonal, flags, 0.0), axis=1, keepdims=True) > 0.5
        own_real = jnp.where(usable, real[SLOT * i : SLOT * (i + 1)], 0.0)
        own_imag = jnp.where(usable, imag[SLOT * i : SLOT * (i + 1)], 0.0)
        trace = iota((8, TRACES), 1)
        row = iota((8, TRACES), 0)
        spread = ((iota((TRACES, 128), 0) >> 3) == (iota((TRACES, 128), 1) & 7)).astype(BF16)
        spare = []
        for shift in (4, 0):
            chosen = jnp.where((trace & 7) == ((row + shift) & 7), flags, 0.0)
            placed = jnp.dot(chosen.astype(BF16), spread, preferred_element_type=F32)
            spare.append(jnp.concatenate([placed] * (BINS // 128), axis=1))
        last = iota((8, BINS), 0) >= 4
        stack = jnp.concatenate(
            [
                own_real[: SLOT - 8],
                jnp.where(last, spare[0], own_real[SLOT - 8 :]),
                own_imag[: SLOT - 8],
                jnp.where(last, spare[1], own_imag[SLOT - 8 :]),
            ],
            axis=0,
        )
        pieces.append(jnp.transpose(stack).reshape(DEVICES, PER, 2 * SLOT))
    out_ref[...] = jnp.concatenate(pieces, axis=1).astype(BF16)


def anywhere(count):
    return [pl.BlockSpec(memory_space=pl.ANY)] * count


def whitened_spectra(traces, masks):
    return pl.pallas_call(
        whiten_kernel,
        in_specs=anywhere(4),
        out_shape=jax.ShapeDtypeStruct((DEVICES, OWN * PER, 2 * SLOT), BF16),
        scratch_shapes=[
            pltpu.VMEM((OWN, TRACES, SAMPLES), BF16),
            pltpu.VMEM((OWN, TRACES), jnp.int32),
            pltpu.VMEM((4, QUARTER, 2 * CLASS), BF16),
            pltpu.VMEM((8, BINS), F32),
            pltpu.VMEM((4, 2 * OWN * SLOT, QUARTER), BF16),
            pltpu.SemaphoreType.DMA((9,)),
        ],
        compiler_params=pltpu.CompilerParams(vmem_limit_bytes=60 * MIB),
        name="whiten",
    )(traces, masks, jnp.asarray(forward_tables()), jnp.asarray(window_rows()))


def cross_kernel(got_ref, out_ref, own_ref, sorted_ref, scale_ref, part_ref):
    lanes = 2 * SLOT
    block = CHANNELS // COLS
    own_ref[...] = got_ref[...].reshape(DEVICES * OWN * PER, lanes).astype(F32)
    lane = iota((CHANNELS, lanes), 1)
    spare = (lane & (SLOT - 1)) >= TRACES
    sign = jnp.where(lane < SLOT, 1.0, -1.0)
    flags = jnp.zeros((CHANNELS, lanes), F32)
    for j in range(PER):
        for i in range(OWN):
            value = own_ref[pl.ds(i * PER + j, DEVICES, stride=OWN * PER), :]
            sorted_ref[j, pl.ds(i, DEVICES, stride=OWN), :] = value
        extra = jnp.where(spare, sorted_ref[j], 0.0)
        flags += pltpu.roll(extra, 4 * j, 1) if j else extra
    flags = flags.astype(BF16)
    tallies = lax.dot_general(flags, flags, NT, preferred_element_type=F32)
    scale_ref[...] = 1.0 / jnp.maximum(tallies, 1.0)
    for j in range(PER):
        right = sorted_ref[j]
        left = jnp.where(spare, 0.0, right)
        left = jnp.concatenate([left, pltpu.roll(left, SLOT, 1) * sign], axis=0)
        cross = lax.dot_general(
            left.astype(BF16), right.astype(BF16), NT, preferred_element_type=F32
        )
        for t in range(CHANNELS // 128):
            for p in range(2):
                part_ref[t, pl.ds(PER * p + j, CHANNELS, stride=2 * PER), :] = (
                    cross[CHANNELS * p : CHANNELS * (p + 1), 128 * t : 128 * (t + 1)]
                    * scale_ref[:, 128 * t : 128 * (t + 1)]
                )

    where = iota((2 * PER, CHANNELS), 1) // block
    bits = [(where >> k) & 1 == 1 for k in range(4)]

    def one_row(g, carry):
        parts = []
        for s in range(COLS):
            channel = (g % ROWS) * OWN * COLS + OWN * s + g // ROWS
            rows = pl.ds(pl.multiple_of(channel * 2 * PER, 2 * PER), 2 * PER)
            value = jnp.concatenate(
                [part_ref[t, rows, :] for t in range(CHANNELS // 128)], axis=1
            )
            value = value.astype(BF16)
            parts.append(pltpu.roll(value, block * s, 1) if s else value)
        for t in range(CHANNELS // 128):
            cut = slice(128 * t, 128 * (t + 1))
            tiles = [part[:, cut] for part in parts]
            for k in range(4):
                tiles = [
                    jnp.where(bits[k][:, cut], tiles[(s + (1 << k)) % COLS], tiles[s])
                    for s in range(COLS)
                ]
            for c in range(COLS):
                lanes_of = pl.ds(pl.multiple_of(g // ROWS * CHANNELS + 128 * t, 128), 128)
                out_ref[g % ROWS * COLS + c, :, lanes_of] = tiles[-c % COLS]
        return carry

    lax.fori_loop(0, OWN * ROWS, one_row, 0, unroll=3)


def cross_spectra(got):
    return pl.pallas_call(
        cross_kernel,
        out_shape=jax.ShapeDtypeStruct((DEVICES, 2 * PER, OWN * CHANNELS), BF16),
        scratch_shapes=[
            pltpu.VMEM((DEVICES * OWN * PER, 2 * SLOT), F32),
            pltpu.VMEM((PER, CHANNELS, 2 * SLOT), F32),
            pltpu.VMEM((CHANNELS, CHANNELS), F32),
            pltpu.VMEM((CHANNELS // 128, CHANNELS * 2 * PER, 128), F32),
        ],
        compiler_params=pltpu.CompilerParams(vmem_limit_bytes=32 * MIB),
        name="cross",
    )(got)


LAG_STEP = 512
HALF = LAGS // 2


def lag_kernel(x_ref, table_ref, edge_ref, out_hbm, out_ref, sems):
    block = CHANNELS // COLS
    steps = HALF // LAG_STEP
    col = lax.axis_index("col")

    def store(i, first, value):
        width = value.shape[1]
        for place in range(COLS):
            source = (place + COLS - col) % COLS
            out_ref[i, source, :, first : first + width] = value[block * place : block * (place + 1)]

    copies = []

    def send(i, first):
        copy = pltpu.make_async_copy(
            out_ref.at[i, :, :, pl.ds(first, LAG_STEP)],
            out_hbm.at[:, i, :, pl.ds(first, LAG_STEP)],
            sems.at[len(copies)],
        )
        copy.start()
        copies.append(copy)

    lane = iota((CHANNELS, 128), 1)
    mirror = (128 - lane) & 127
    for i in range(OWN):
        parts = []
        for p in range(2):
            rows = x_ref[:, PER * p : PER * (p + 1), CHANNELS * i : CHANNELS * (i + 1)]
            rows = rows.astype(F32).reshape(BINS, CHANNELS)
            parts.append(jnp.transpose(rows))
        edge = jnp.sum(
            parts[0] * edge_ref[0:1, :] + parts[1] * edge_ref[1:2, :], axis=1, keepdims=True
        )
        real, imag = parts[0].astype(BF16), parts[1].astype(BF16)
        before = jnp.broadcast_to(edge, (CHANNELS, 128))
        for n in reversed(range(steps)):
            even = jnp.dot(real, table_ref[n, 0], preferred_element_type=F32)
            odd = jnp.dot(imag, table_ref[n, 1], preferred_element_type=F32)
            store(i, HALF + LAG_STEP * n, even + odd)
            send(i, HALF + LAG_STEP * n)
            back = even - odd
            for t in reversed(range(LAG_STEP // 128)):
                turned = jnp.take_along_axis(back[:, 128 * t : 128 * (t + 1)], mirror, axis=1)
                first = HALF - LAG_STEP * n - 128 * (t + 1)
                store(i, first, jnp.where(lane == 0, before, turned))
                before = turned
            send(i, HALF - LAG_STEP * (n + 1))
    for copy in copies:
        copy.wait()


def split_lag_tables():
    table, edge = lag_tables()
    steps = HALF // LAG_STEP
    table = table.reshape(2, BINS, steps, LAG_STEP).transpose(2, 0, 1, 3)
    return jnp.asarray(table), jnp.asarray(edge)


def correlations_of(stacked, table, edge):
    block = CHANNELS // COLS
    steps = HALF // LAG_STEP
    return pl.pallas_call(
        lag_kernel,
        in_specs=[
            *[pl.BlockSpec(memory_space=pltpu.VMEM)] * 3,
        ],
        out_specs=pl.BlockSpec(memory_space=pl.ANY),
        out_shape=jax.ShapeDtypeStruct((COLS, OWN, block, LAGS), F32),
        scratch_shapes=[
            pltpu.VMEM((OWN, COLS, block, LAGS), F32),
            pltpu.SemaphoreType.DMA((2 * OWN * steps,)),
        ],
        compiler_params=pltpu.CompilerParams(vmem_limit_bytes=36 * MIB),
        name="lags",
    )(stacked, table, edge)


def local(traces, masks):
    axes = ("row", "col")
    spectra = whitened_spectra(traces, masks)
    by_bin = lax.all_to_all(spectra, axes, 0, 0, tiled=True)
    stacked = cross_spectra(by_bin)
    table, edge = split_lag_tables()
    by_pair = lax.all_to_all(stacked, axes, 0, 0, tiled=True)
    result = correlations_of(by_pair, table, edge)
    return result.reshape(OWN * COLS, CHANNELS // COLS, LAGS)


def solution(mesh):
    in_specs = (P(("row", "col"), None, None), P(("row", "col"), None))
    out_specs = P("row", "col", None)
    return jax.shard_map(local, mesh=mesh, in_specs=in_specs, out_specs=out_specs, check_vma=False)
```

```python
import math

import jax
import jax.numpy as jnp
import ml_dtypes
import numpy as np
from jax import lax
from jax.experimental import pallas as pl
from jax.experimental.pallas import tpu as pltpu
from jax.sharding import PartitionSpec as P

TRACES = 60
SAMPLES = 8192
BINS = 1024
LOW_BIN = 33
LAGS = 2048
SMOOTH = 64
EDGE = 64

F32 = jnp.float32
BF16 = jnp.bfloat16
MIB = 1 << 20

OWN = 3
SLOT = 64
QUARTER = SAMPLES // 4
CLASS = BINS // 4
PER = 8
DEVICES = BINS // PER
ROWS = 8
COLS = 16
CHANNELS = OWN * DEVICES
NT = (((1,), (1,)), ((), ()))


def bin_order():
    k = np.arange(BINS)
    return np.concatenate([k[(k + LOW_BIN) % 4 == q] for q in range(4)])


def angles_of(phases):
    return (phases % SAMPLES).astype(np.float32) * np.float32(2.0 * math.pi / SAMPLES)


def cosine(angles):
    return np.cos(angles.astype(np.float64)).astype(np.float32)


def sine(angles):
    return np.sin(angles.astype(np.float64)).astype(np.float32)


def forward_tables():
    bins = (LOW_BIN + bin_order()).reshape(4, 1, CLASS)
    angles = angles_of(np.arange(QUARTER).reshape(1, QUARTER, 1) * bins)
    return np.concatenate([cosine(angles), -sine(angles)], axis=2).astype(ml_dtypes.bfloat16)


def lag_tables():
    bins = LOW_BIN + bin_order()
    factor = np.float32(2.0 / math.sqrt(BINS))

    def at(lags):
        angles = angles_of(bins[:, None] * (lags[None, :] + SAMPLES))
        both = factor * np.stack([cosine(angles), -sine(angles)])
        return both.astype(ml_dtypes.bfloat16)

    edge = np.zeros((8, BINS), np.float32)
    edge[:2] = at(np.array([-LAGS // 2]))[:, :, 0].astype(np.float32)
    return at(np.arange(LAGS // 2)), edge


def window_rows():
    order = bin_order()
    nearby = np.abs(order[:, None] - order[None, :]) <= SMOOTH
    distance = np.minimum(order, BINS - 1 - order).astype(np.float32)
    ramp = np.minimum((distance + np.float32(0.5)) / np.float32(EDGE), np.float32(1.0))
    taper = np.float32(0.5) - np.float32(0.5) * cosine(np.float32(math.pi) * ramp)
    rows = np.zeros((8, BINS), np.float32)
    rows[0] = taper
    rows[1] = np.float32(1.0) / nearby.sum(axis=0).astype(np.float32)
    return rows


def iota(shape, axis):
    return lax.broadcasted_iota(jnp.int32, shape, axis)


def halves(value):
    high = value.astype(BF16)
    return high, (value - high.astype(F32)).astype(BF16)


def whiten_kernel(
    x_hbm, m_hbm, table_hbm, rows_hbm, out_ref, x_ref, m_ref, table_ref, rows_ref, u_ref, sems
):
    span = OWN * SLOT
    order = (0, 2, 1, 3)
    x_copies = [
        pltpu.make_async_copy(x_hbm.at[i], x_ref.at[i], sems.at[i]) for i in range(OWN)
    ]
    table_copies = {
        q: pltpu.make_async_copy(table_hbm.at[q], table_ref.at[q], sems.at[OWN + q]) for q in order
    }
    last_copies = [
        pltpu.make_async_copy(m_hbm, m_ref, sems.at[7]),
        pltpu.make_async_copy(rows_hbm, rows_ref, sems.at[8]),
    ]
    for copy in (*x_copies, *table_copies.values(), *last_copies):
        copy.start()
    for copy in x_copies:
        copy.wait()

    for i in range(OWN):
        part = [x_ref[i, :, QUARTER * j : QUARTER * (j + 1)].astype(F32) for j in range(4)]
        even, odd = part[0] + part[2], part[1] + part[3]
        kinds = (even + odd, even - odd, part[0] - part[2], part[1] - part[3])
        for kind, value in enumerate(kinds):
            high, low = halves(value)
            u_ref[kind, SLOT * i : SLOT * i + TRACES, :] = high
            u_ref[kind, span + SLOT * i : span + SLOT * i + TRACES, :] = low

    def times_table(kind, q):
        both = jnp.dot(u_ref[kind], table_ref[q], preferred_element_type=F32)
        both = both[:span] + both[span:]
        return both[:, :CLASS], both[:, CLASS:]

    reals, imags = {}, {}
    for q in order:
        if q == 0:
            table_copies[0].wait()
            table_copies[2].wait()
        if q == 1:
            for copy in (table_copies[1], table_copies[3], *last_copies):
                copy.wait()
        if q % 2 == 0:
            reals[q], imags[q] = times_table(q // 2, q)
        else:
            first, second = times_table(2, q), times_table(3, q)
            if q == 1:
                reals[q], imags[q] = first[0] + second[1], first[1] - second[0]
            else:
                reals[q], imags[q] = first[0] - second[1], first[1] + second[0]

    place = {c: (c - LOW_BIN) % 4 for c in range(4)}
    by_place = sorted(range(4), key=place.get)
    sizes = {c: jnp.sqrt(reals[c] * reals[c] + imags[c] * imags[c]) for c in range(4)}
    every = sizes[0] + sizes[1] + sizes[2] + sizes[3]
    reach = SMOOTH // 4
    band = jnp.abs(iota((CLASS, CLASS), 0) - iota((CLASS, CLASS), 1)) < reach
    middle = jnp.dot(
        jnp.concatenate(halves(every), axis=0), band.astype(BF16), preferred_element_type=F32
    )
    middle = middle[:span] + middle[span:]
    lane = iota((span, CLASS), 1)
    totals = {}
    upto = jnp.zeros((span, CLASS), F32)
    for c in by_place:
        onward = every - upto
        upto = upto + sizes[c]
        ahead = jnp.where(lane < CLASS - reach, pltpu.roll(upto, CLASS - reach, 1), 0.0)
        behind = jnp.where(lane >= reach, pltpu.roll(onward, reach, 1), 0.0)
        totals[c] = middle + ahead + behind
    total = jnp.concatenate([totals[c] for c in range(4)], axis=1)
    real = jnp.concatenate([reals[q] for q in range(4)], axis=1)
    imag = jnp.concatenate([imags[q] for q in range(4)], axis=1)
    level = total * rows_ref[1:2, :] + 1e-06
    weights = rows_ref[0:1, :] / level
    real = real * weights
    imag = imag * weights
    pieces = []
    for i in range(OWN):
        flags = m_ref[i : i + 1, :].astype(F32)
        square = (SLOT, TRACES)
        diagonal = iota(square, 0) == iota(square, 1)
        usable = jnp.sum(jnp.where(diagonal, flags, 0.0), axis=1, keepdims=True) > 0.5
        own_real = jnp.where(usable, real[SLOT * i : SLOT * (i + 1)], 0.0)
        own_imag = jnp.where(usable, imag[SLOT * i : SLOT * (i + 1)], 0.0)
        trace = iota((8, TRACES), 1)
        row = iota((8, TRACES), 0)
        spread = ((iota((TRACES, 128), 0) >> 3) == (iota((TRACES, 128), 1) & 7)).astype(BF16)
        spare = []
        for shift in (4, 0):
            chosen = jnp.where((trace & 7) == ((row + shift) & 7), flags, 0.0)
            placed = jnp.dot(chosen.astype(BF16), spread, preferred_element_type=F32)
            spare.append(jnp.concatenate([placed] * (BINS // 128), axis=1))
        last = iota((8, BINS), 0) >= 4
        stack = jnp.concatenate(
            [
                own_real[: SLOT - 8],
                jnp.where(last, spare[0], own_real[SLOT - 8 :]),
                own_imag[: SLOT - 8],
                jnp.where(last, spare[1], own_imag[SLOT - 8 :]),
            ],
            axis=0,
        )
        pieces.append(jnp.transpose(stack).reshape(DEVICES, PER, 2 * SLOT))
    out_ref[...] = jnp.concatenate(pieces, axis=1).astype(BF16)


def anywhere(count):
    return [pl.BlockSpec(memory_space=pl.ANY)] * count


def in_hbm(array):
    return pltpu.with_memory_space_constraint(array, pltpu.HBM)


def whitened_spectra(traces, masks):
    operands = (traces, masks, jnp.asarray(forward_tables()), jnp.asarray(window_rows()))
    return pl.pallas_call(
        whiten_kernel,
        in_specs=anywhere(4),
        out_shape=jax.ShapeDtypeStruct((DEVICES, OWN * PER, 2 * SLOT), BF16),
        scratch_shapes=[
            pltpu.VMEM((OWN, TRACES, SAMPLES), BF16),
            pltpu.VMEM((OWN, TRACES), jnp.int32),
            pltpu.VMEM((4, QUARTER, 2 * CLASS), BF16),
            pltpu.VMEM((8, BINS), F32),
            pltpu.VMEM((4, 2 * OWN * SLOT, QUARTER), BF16),
            pltpu.SemaphoreType.DMA((9,)),
        ],
        compiler_params=pltpu.CompilerParams(vmem_limit_bytes=40 * MIB),
        name="whiten",
    )(*(in_hbm(array) for array in operands))


def cross_kernel(got_ref, out_ref, own_ref, sorted_ref, scale_ref, part_ref):
    lanes = 2 * SLOT
    block = CHANNELS // COLS
    own_ref[...] = got_ref[...].reshape(DEVICES * OWN * PER, lanes).astype(F32)
    lane = iota((CHANNELS, lanes), 1)
    spare = (lane & (SLOT - 1)) >= TRACES
    sign = jnp.where(lane < SLOT, 1.0, -1.0)
    flags = jnp.zeros((CHANNELS, lanes), F32)
    for j in range(PER):
        for i in range(OWN):
            value = own_ref[pl.ds(i * PER + j, DEVICES, stride=OWN * PER), :]
            sorted_ref[j, pl.ds(i, DEVICES, stride=OWN), :] = value
        extra = jnp.where(spare, sorted_ref[j], 0.0)
        flags += pltpu.roll(extra, 4 * j, 1) if j else extra
    flags = flags.astype(BF16)
    tallies = lax.dot_general(flags, flags, NT, preferred_element_type=F32)
    scale_ref[...] = 1.0 / jnp.maximum(tallies, 1.0)
    for j in range(PER):
        right = sorted_ref[j]
        left = jnp.where(spare, 0.0, right)
        left = jnp.concatenate([left, pltpu.roll(left, SLOT, 1) * sign], axis=0)
        cross = lax.dot_general(
            left.astype(BF16), right.astype(BF16), NT, preferred_element_type=F32
        )
        for t in range(CHANNELS // 128):
            for p in range(2):
                part_ref[t, pl.ds(PER * p + j, CHANNELS, stride=2 * PER), :] = (
                    cross[CHANNELS * p : CHANNELS * (p + 1), 128 * t : 128 * (t + 1)]
                    * scale_ref[:, 128 * t : 128 * (t + 1)]
                )

    where = iota((2 * PER, CHANNELS), 1) // block
    bits = [(where >> k) & 1 == 1 for k in range(4)]

    def one_row(g, carry):
        parts = []
        for s in range(COLS):
            channel = (g % ROWS) * OWN * COLS + OWN * s + g // ROWS
            rows = pl.ds(pl.multiple_of(channel * 2 * PER, 2 * PER), 2 * PER)
            value = jnp.concatenate(
                [part_ref[t, rows, :] for t in range(CHANNELS // 128)], axis=1
            )
            value = value.astype(BF16)
            parts.append(pltpu.roll(value, block * s, 1) if s else value)
        for t in range(CHANNELS // 128):
            cut = slice(128 * t, 128 * (t + 1))
            tiles = [part[:, cut] for part in parts]
            for k in range(4):
                tiles = [
                    jnp.where(bits[k][:, cut], tiles[(s + (1 << k)) % COLS], tiles[s])
                    for s in range(COLS)
                ]
            for c in range(COLS):
                lanes_of = pl.ds(pl.multiple_of(g // ROWS * CHANNELS + 128 * t, 128), 128)
                out_ref[g % ROWS * COLS + c, :, lanes_of] = tiles[-c % COLS]
        return carry

    lax.fori_loop(0, OWN * ROWS, one_row, 0, unroll=6)


def cross_spectra(got):
    return pl.pallas_call(
        cross_kernel,
        out_shape=jax.ShapeDtypeStruct((DEVICES, 2 * PER, OWN * CHANNELS), BF16),
        scratch_shapes=[
            pltpu.VMEM((DEVICES * OWN * PER, 2 * SLOT), F32),
            pltpu.VMEM((PER, CHANNELS, 2 * SLOT), F32),
            pltpu.VMEM((CHANNELS, CHANNELS), F32),
            pltpu.VMEM((CHANNELS // 128, CHANNELS * 2 * PER, 128), F32),
        ],
        compiler_params=pltpu.CompilerParams(vmem_limit_bytes=32 * MIB),
        name="cross",
    )(got)


LAG_STEP = 512
HALF = LAGS // 2


def lag_kernel(x_ref, table_ref, edge_ref, out_hbm, out_ref, sems):
    block = CHANNELS // COLS
    steps = HALF // LAG_STEP
    col = lax.axis_index("col")

    def store(i, first, value):
        width = value.shape[1]
        for place in range(COLS):
            source = (place + COLS - col) % COLS
            out_ref[i, source, :, first : first + width] = value[block * place : block * (place + 1)]

    copies = []

    def send(i, first, width):
        copy = pltpu.make_async_copy(
            out_ref.at[i, :, :, pl.ds(first, width)],
            out_hbm.at[:, i, :, pl.ds(first, width)],
            sems.at[len(copies)],
        )
        copy.start()
        copies.append(copy)

    lane = iota((CHANNELS, 128), 1)
    mirror = (128 - lane) & 127
    for i in range(OWN):
        parts = []
        for p in range(2):
            rows = x_ref[:, PER * p : PER * (p + 1), CHANNELS * i : CHANNELS * (i + 1)]
            rows = rows.astype(F32).reshape(BINS, CHANNELS)
            parts.append(jnp.transpose(rows))
        edge = jnp.sum(
            parts[0] * edge_ref[0:1, :] + parts[1] * edge_ref[1:2, :], axis=1, keepdims=True
        )
        real, imag = parts[0].astype(BF16), parts[1].astype(BF16)
        before = jnp.broadcast_to(edge, (CHANNELS, 128))
        for n in reversed(range(steps)):
            even = jnp.dot(real, table_ref[n, 0], preferred_element_type=F32)
            odd = jnp.dot(imag, table_ref[n, 1], preferred_element_type=F32)
            store(i, HALF + LAG_STEP * n, even + odd)
            back = even - odd
            for t in reversed(range(LAG_STEP // 128)):
                turned = jnp.take_along_axis(back[:, 128 * t : 128 * (t + 1)], mirror, axis=1)
                first = HALF - LAG_STEP * n - 128 * (t + 1)
                store(i, first, jnp.where(lane == 0, before, turned))
                before = turned
            if i == OWN - 1:
                send(i, HALF + LAG_STEP * n, LAG_STEP)
                send(i, HALF - LAG_STEP * (n + 1), LAG_STEP)
        if i < OWN - 1:
            send(i, 0, LAGS)
    for copy in copies:
        copy.wait()


def split_lag_tables():
    table, edge = lag_tables()
    steps = HALF // LAG_STEP
    table = table.reshape(2, BINS, steps, LAG_STEP).transpose(2, 0, 1, 3)
    return jnp.asarray(table), jnp.asarray(edge)


def correlations_of(stacked, table, edge):
    block = CHANNELS // COLS
    steps = HALF // LAG_STEP
    return pl.pallas_call(
        lag_kernel,
        in_specs=[
            *[pl.BlockSpec(memory_space=pltpu.VMEM)] * 3,
        ],
        out_specs=pl.BlockSpec(memory_space=pl.ANY),
        out_shape=jax.ShapeDtypeStruct((COLS, OWN, block, LAGS), F32),
        scratch_shapes=[
            pltpu.VMEM((OWN, COLS, block, LAGS), F32),
            pltpu.SemaphoreType.DMA((2 * OWN * steps,)),
        ],
        compiler_params=pltpu.CompilerParams(vmem_limit_bytes=36 * MIB),
        name="lags",
    )(stacked, table, edge)


def local(traces, masks):
    axes = ("row", "col")
    spectra = whitened_spectra(traces, masks)
    by_bin = lax.all_to_all(spectra, axes, 0, 0, tiled=True)
    stacked = cross_spectra(by_bin)
    table, edge = split_lag_tables()
    by_pair = lax.all_to_all(stacked, axes, 0, 0, tiled=True)
    result = correlations_of(by_pair, table, edge)
    return result.reshape(OWN * COLS, CHANNELS // COLS, LAGS)


def solution(mesh):
    in_specs = (P(("row", "col"), None, None), P(("row", "col"), None))
    out_specs = P("row", "col", None)
    return jax.shard_map(local, mesh=mesh, in_specs=in_specs, out_specs=out_specs, check_vma=False)
```

```python
import math

import jax
import jax.numpy as jnp
import ml_dtypes
import numpy as np
from jax import lax
from jax.experimental import pallas as pl
from jax.experimental.pallas import tpu as pltpu
from jax.sharding import PartitionSpec as P

TRACES = 60
SAMPLES = 8192
BINS = 1024
LOW_BIN = 33
LAGS = 2048
SMOOTH = 64
EDGE = 64

F32 = jnp.float32
BF16 = jnp.bfloat16
MIB = 1 << 20

OWN = 3
SLOT = 64
QUARTER = SAMPLES // 4
CLASS = BINS // 4
PER = 8
DEVICES = BINS // PER
ROWS = 8
COLS = 16
CHANNELS = OWN * DEVICES
NT = (((1,), (1,)), ((), ()))


def bin_order():
    k = np.arange(BINS)
    return np.concatenate([k[(k + LOW_BIN) % 4 == q] for q in range(4)])


def angles_of(phases):
    return (phases % SAMPLES).astype(np.float32) * np.float32(2.0 * math.pi / SAMPLES)


def cosine(angles):
    return np.cos(angles.astype(np.float64)).astype(np.float32)


def sine(angles):
    return np.sin(angles.astype(np.float64)).astype(np.float32)


def forward_tables():
    bins = (LOW_BIN + bin_order()).reshape(4, 1, CLASS)
    angles = angles_of(np.arange(QUARTER).reshape(1, QUARTER, 1) * bins)
    return np.concatenate([cosine(angles), -sine(angles)], axis=2).astype(ml_dtypes.bfloat16)


def lag_tables():
    bins = LOW_BIN + bin_order()
    factor = np.float32(2.0 / math.sqrt(BINS))

    def at(lags):
        angles = angles_of(bins[:, None] * (lags[None, :] + SAMPLES))
        both = factor * np.stack([cosine(angles), -sine(angles)])
        return both.astype(ml_dtypes.bfloat16)

    edge = np.zeros((8, BINS), np.float32)
    edge[:2] = at(np.array([-LAGS // 2]))[:, :, 0].astype(np.float32)
    return at(np.arange(LAGS // 2)), edge


def window_rows():
    order = bin_order()
    nearby = np.abs(order[:, None] - order[None, :]) <= SMOOTH
    distance = np.minimum(order, BINS - 1 - order).astype(np.float32)
    ramp = np.minimum((distance + np.float32(0.5)) / np.float32(EDGE), np.float32(1.0))
    taper = np.float32(0.5) - np.float32(0.5) * cosine(np.float32(math.pi) * ramp)
    rows = np.zeros((8, BINS), np.float32)
    rows[0] = taper
    rows[1] = np.float32(1.0) / nearby.sum(axis=0).astype(np.float32)
    return rows


def iota(shape, axis):
    return lax.broadcasted_iota(jnp.int32, shape, axis)


def halves(value):
    high = value.astype(BF16)
    return high, (value - high.astype(F32)).astype(BF16)


def whiten_kernel(
    x_hbm, m_hbm, table_hbm, rows_hbm, out_ref, x_ref, m_ref, table_ref, rows_ref, u_ref, sems
):
    span = OWN * SLOT
    order = (0, 2, 1, 3)
    x_copies = [
        pltpu.make_async_copy(x_hbm.at[i], x_ref.at[i], sems.at[i]) for i in range(OWN)
    ]
    table_copies = {
        q: pltpu.make_async_copy(table_hbm.at[q], table_ref.at[q], sems.at[OWN + q]) for q in order
    }
    last_copies = [
        pltpu.make_async_copy(m_hbm, m_ref, sems.at[7]),
        pltpu.make_async_copy(rows_hbm, rows_ref, sems.at[8]),
    ]
    for copy in (*x_copies, *table_copies.values(), *last_copies):
        copy.start()
    for copy in x_copies:
        copy.wait()

    for i in range(OWN):
        part = [x_ref[i, :, QUARTER * j : QUARTER * (j + 1)].astype(F32) for j in range(4)]
        even, odd = part[0] + part[2], part[1] + part[3]
        for kind, value in enumerate((even + odd, even - odd)):
            high, low = halves(value)
            u_ref[kind, SLOT * i : SLOT * i + TRACES, :] = high
            u_ref[kind, span + SLOT * i : span + SLOT * i + TRACES, :] = low
        for j in range(4):
            first = span * (j // 2) + SLOT * i
            u_ref[2 + j % 2, first : first + TRACES, :] = x_ref[
                i, :, QUARTER * j : QUARTER * (j + 1)
            ]

    def times_table(kind, q):
        both = jnp.dot(u_ref[kind], table_ref[q], preferred_element_type=F32)
        both = both[:span] + both[span:] if kind < 2 else both[:span] - both[span:]
        return both[:, :CLASS], both[:, CLASS:]

    reals, imags = {}, {}
    for q in order:
        if q == 0:
            table_copies[0].wait()
            table_copies[2].wait()
        if q == 1:
            for copy in (table_copies[1], table_copies[3], *last_copies):
                copy.wait()
        if q % 2 == 0:
            reals[q], imags[q] = times_table(q // 2, q)
        else:
            first, second = times_table(2, q), times_table(3, q)
            if q == 1:
                reals[q], imags[q] = first[0] + second[1], first[1] - second[0]
            else:
                reals[q], imags[q] = first[0] - second[1], first[1] + second[0]

    place = {c: (c - LOW_BIN) % 4 for c in range(4)}
    by_place = sorted(range(4), key=place.get)
    sizes = {c: jnp.sqrt(reals[c] * reals[c] + imags[c] * imags[c]) for c in range(4)}
    every = sizes[0] + sizes[1] + sizes[2] + sizes[3]
    reach = SMOOTH // 4
    band = jnp.abs(iota((CLASS, CLASS), 0) - iota((CLASS, CLASS), 1)) < reach
    middle = jnp.dot(
        jnp.concatenate(halves(every), axis=0), band.astype(BF16), preferred_element_type=F32
    )
    middle = middle[:span] + middle[span:]
    lane = iota((span, CLASS), 1)
    totals = {}
    upto = jnp.zeros((span, CLASS), F32)
    for c in by_place:
        onward = every - upto
        upto = upto + sizes[c]
        ahead = jnp.where(lane < CLASS - reach, pltpu.roll(upto, CLASS - reach, 1), 0.0)
        behind = jnp.where(lane >= reach, pltpu.roll(onward, reach, 1), 0.0)
        totals[c] = middle + ahead + behind
    total = jnp.concatenate([totals[c] for c in range(4)], axis=1)
    real = jnp.concatenate([reals[q] for q in range(4)], axis=1)
    imag = jnp.concatenate([imags[q] for q in range(4)], axis=1)
    level = total * rows_ref[1:2, :] + 1e-06
    weights = rows_ref[0:1, :] / level
    real = real * weights
    imag = imag * weights
    pieces = []
    for i in range(OWN):
        flags = m_ref[i : i + 1, :].astype(F32)
        square = (SLOT, TRACES)
        diagonal = iota(square, 0) == iota(square, 1)
        usable = jnp.sum(jnp.where(diagonal, flags, 0.0), axis=1, keepdims=True) > 0.5
        own_real = jnp.where(usable, real[SLOT * i : SLOT * (i + 1)], 0.0)
        own_imag = jnp.where(usable, imag[SLOT * i : SLOT * (i + 1)], 0.0)
        trace = iota((8, TRACES), 1)
        row = iota((8, TRACES), 0)
        spread = ((iota((TRACES, 128), 0) >> 3) == (iota((TRACES, 128), 1) & 7)).astype(BF16)
        spare = []
        for shift in (4, 0):
            chosen = jnp.where((trace & 7) == ((row + shift) & 7), flags, 0.0)
            placed = jnp.dot(chosen.astype(BF16), spread, preferred_element_type=F32)
            spare.append(jnp.concatenate([placed] * (BINS // 128), axis=1))
        last = iota((8, BINS), 0) >= 4
        stack = jnp.concatenate(
            [
                own_real[: SLOT - 8],
                jnp.where(last, spare[0], own_real[SLOT - 8 :]),
                own_imag[: SLOT - 8],
                jnp.where(last, spare[1], own_imag[SLOT - 8 :]),
            ],
            axis=0,
        )
        pieces.append(jnp.transpose(stack).reshape(DEVICES, PER, 2 * SLOT))
    out_ref[...] = jnp.concatenate(pieces, axis=1).astype(BF16)


def anywhere(count):
    return [pl.BlockSpec(memory_space=pl.ANY)] * count


def in_hbm(array):
    return pltpu.with_memory_space_constraint(array, pltpu.HBM)


def whitened_spectra(traces, masks):
    operands = (traces, masks, jnp.asarray(forward_tables()), jnp.asarray(window_rows()))
    return pl.pallas_call(
        whiten_kernel,
        in_specs=anywhere(4),
        out_shape=jax.ShapeDtypeStruct((DEVICES, OWN * PER, 2 * SLOT), BF16),
        scratch_shapes=[
            pltpu.VMEM((OWN, TRACES, SAMPLES), BF16),
            pltpu.VMEM((OWN, TRACES), jnp.int32),
            pltpu.VMEM((4, QUARTER, 2 * CLASS), BF16),
            pltpu.VMEM((8, BINS), F32),
            pltpu.VMEM((4, 2 * OWN * SLOT, QUARTER), BF16),
            pltpu.SemaphoreType.DMA((9,)),
        ],
        compiler_params=pltpu.CompilerParams(vmem_limit_bytes=40 * MIB),
        name="whiten",
    )(*(in_hbm(array) for array in operands))


def cross_kernel(got_ref, out_ref, own_ref, sorted_ref, scale_ref, part_ref):
    lanes = 2 * SLOT
    block = CHANNELS // COLS
    own_ref[...] = got_ref[...].reshape(DEVICES * OWN * PER, lanes).astype(F32)
    lane = iota((CHANNELS, lanes), 1)
    spare = (lane & (SLOT - 1)) >= TRACES
    sign = jnp.where(lane < SLOT, 1.0, -1.0)
    flags = jnp.zeros((CHANNELS, lanes), F32)
    for j in range(PER):
        for i in range(OWN):
            value = own_ref[pl.ds(i * PER + j, DEVICES, stride=OWN * PER), :]
            sorted_ref[j, pl.ds(i, DEVICES, stride=OWN), :] = value
        extra = jnp.where(spare, sorted_ref[j], 0.0)
        flags += pltpu.roll(extra, 4 * j, 1) if j else extra
    flags = flags.astype(BF16)
    tallies = lax.dot_general(flags, flags, NT, preferred_element_type=F32)
    scale_ref[...] = 1.0 / jnp.maximum(tallies, 1.0)
    for j in range(PER):
        right = sorted_ref[j]
        left = jnp.where(spare, 0.0, right)
        left = jnp.concatenate([left, pltpu.roll(left, SLOT, 1) * sign], axis=0)
        cross = lax.dot_general(
            left.astype(BF16), right.astype(BF16), NT, preferred_element_type=F32
        )
        for t in range(CHANNELS // 128):
            for p in range(2):
                part_ref[t, pl.ds(PER * p + j, CHANNELS, stride=2 * PER), :] = (
                    cross[CHANNELS * p : CHANNELS * (p + 1), 128 * t : 128 * (t + 1)]
                    * scale_ref[:, 128 * t : 128 * (t + 1)]
                )

    where = iota((2 * PER, CHANNELS), 1) // block
    bits = [(where >> k) & 1 == 1 for k in range(4)]

    def one_row(g, carry):
        parts = []
        for s in range(COLS):
            channel = (g % ROWS) * OWN * COLS + OWN * s + g // ROWS
            rows = pl.ds(pl.multiple_of(channel * 2 * PER, 2 * PER), 2 * PER)
            value = jnp.concatenate(
                [part_ref[t, rows, :] for t in range(CHANNELS // 128)], axis=1
            )
            value = value.astype(BF16)
            parts.append(pltpu.roll(value, block * s, 1) if s else value)
        for t in range(CHANNELS // 128):
            cut = slice(128 * t, 128 * (t + 1))
            tiles = [part[:, cut] for part in parts]
            for k in range(4):
                tiles = [
                    jnp.where(bits[k][:, cut], tiles[(s + (1 << k)) % COLS], tiles[s])
                    for s in range(COLS)
                ]
            for c in range(COLS):
                lanes_of = pl.ds(pl.multiple_of(g // ROWS * CHANNELS + 128 * t, 128), 128)
                out_ref[g % ROWS * COLS + c, :, lanes_of] = tiles[-c % COLS]
        return carry

    lax.fori_loop(0, OWN * ROWS, one_row, 0, unroll=6)


def cross_spectra(got):
    return pl.pallas_call(
        cross_kernel,
        out_shape=jax.ShapeDtypeStruct((DEVICES, 2 * PER, OWN * CHANNELS), BF16),
        scratch_shapes=[
            pltpu.VMEM((DEVICES * OWN * PER, 2 * SLOT), F32),
            pltpu.VMEM((PER, CHANNELS, 2 * SLOT), F32),
            pltpu.VMEM((CHANNELS, CHANNELS), F32),
            pltpu.VMEM((CHANNELS // 128, CHANNELS * 2 * PER, 128), F32),
        ],
        compiler_params=pltpu.CompilerParams(vmem_limit_bytes=32 * MIB),
        name="cross",
    )(got)


LAG_STEP = 512
HALF = LAGS // 2


def lag_kernel(x_ref, table_ref, edge_ref, out_hbm, out_ref, sems):
    block = CHANNELS // COLS
    steps = HALF // LAG_STEP
    col = lax.axis_index("col")

    def store(i, first, value):
        width = value.shape[1]
        for place in range(COLS):
            source = (place + COLS - col) % COLS
            out_ref[i, source, :, first : first + width] = value[block * place : block * (place + 1)]

    copies = []

    def send(i, first, width):
        copy = pltpu.make_async_copy(
            out_ref.at[i, :, :, pl.ds(first, width)],
            out_hbm.at[:, i, :, pl.ds(first, width)],
            sems.at[len(copies)],
        )
        copy.start()
        copies.append(copy)

    lane = iota((CHANNELS, 128), 1)
    mirror = (128 - lane) & 127
    for i in range(OWN):
        parts = []
        for p in range(2):
            rows = x_ref[:, PER * p : PER * (p + 1), CHANNELS * i : CHANNELS * (i + 1)]
            rows = rows.astype(F32).reshape(BINS, CHANNELS)
            parts.append(jnp.transpose(rows))
        edge = jnp.sum(
            parts[0] * edge_ref[0:1, :] + parts[1] * edge_ref[1:2, :], axis=1, keepdims=True
        )
        real, imag = parts[0].astype(BF16), parts[1].astype(BF16)
        before = jnp.broadcast_to(edge, (CHANNELS, 128))
        for n in reversed(range(steps)):
            even = jnp.dot(real, table_ref[n, 0], preferred_element_type=F32)
            odd = jnp.dot(imag, table_ref[n, 1], preferred_element_type=F32)
            store(i, HALF + LAG_STEP * n, even + odd)
            back = even - odd
            for t in reversed(range(LAG_STEP // 128)):
                turned = jnp.take_along_axis(back[:, 128 * t : 128 * (t + 1)], mirror, axis=1)
                first = HALF - LAG_STEP * n - 128 * (t + 1)
                store(i, first, jnp.where(lane == 0, before, turned))
                before = turned
            if i == OWN - 1:
                send(i, HALF + LAG_STEP * n, LAG_STEP)
                send(i, HALF - LAG_STEP * (n + 1), LAG_STEP)
        if i < OWN - 1:
            send(i, 0, LAGS)
    for copy in copies:
        copy.wait()


def split_lag_tables():
    table, edge = lag_tables()
    steps = HALF // LAG_STEP
    table = table.reshape(2, BINS, steps, LAG_STEP).transpose(2, 0, 1, 3)
    return jnp.asarray(table), jnp.asarray(edge)


def correlations_of(stacked, table, edge):
    block = CHANNELS // COLS
    steps = HALF // LAG_STEP
    return pl.pallas_call(
        lag_kernel,
        in_specs=[
            *[pl.BlockSpec(memory_space=pltpu.VMEM)] * 3,
        ],
        out_specs=pl.BlockSpec(memory_space=pl.ANY),
        out_shape=jax.ShapeDtypeStruct((COLS, OWN, block, LAGS), F32),
        scratch_shapes=[
            pltpu.VMEM((OWN, COLS, block, LAGS), F32),
            pltpu.SemaphoreType.DMA((2 * OWN * steps,)),
        ],
        compiler_params=pltpu.CompilerParams(vmem_limit_bytes=36 * MIB),
        name="lags",
    )(stacked, table, edge)


def local(traces, masks):
    axes = ("row", "col")
    spectra = whitened_spectra(traces, masks)
    by_bin = lax.all_to_all(spectra, axes, 0, 0, tiled=True)
    stacked = cross_spectra(by_bin)
    table, edge = split_lag_tables()
    by_pair = lax.all_to_all(stacked, axes, 0, 0, tiled=True)
    result = correlations_of(by_pair, table, edge)
    return result.reshape(OWN * COLS, CHANNELS // COLS, LAGS)


def solution(mesh):
    in_specs = (P(("row", "col"), None, None), P(("row", "col"), None))
    out_specs = P("row", "col", None)
    return jax.shard_map(local, mesh=mesh, in_specs=in_specs, out_specs=out_specs, check_vma=False)
```
